32 devices in a mesh: groups: 2 (over y), dev: 4 (over z), cuts: 4 (over x, core).
Axes of the slice: x: 2, y: 2, z: 4, core: 2. Of those that a mesh axis runs over, the one named last changes fastest.
Arguments:
- residual: bfloat16 [128, 3072], P(('groups', 'dev'), 'cuts'), parts along dimension 0, may hold values from -64 to 64
- queries: bfloat16 [128, 3072], P(('groups', 'dev'), 'cuts'), parts along dimension 0, may hold values from -30 to 30
- keys: bfloat16 [128, 32, 512], P(('groups', 'dev'), None, 'cuts'), parts along dimension 0, may hold values from -12 to 12
- values: bfloat16 [128, 32, 512], P(('groups', 'dev'), None, 'cuts'), parts along dimension 0, may hold values from -12 to 12
- lengths: int32 [128], P(('groups', 'dev')), parts along dimension 0, may hold values from 2 to 32, as said below
- norm_gain: float32 [3072], P('cuts'), may hold values from 0.1 to 1.9
- expert_ids: int32 [128, 2], P(('groups', 'dev')), parts along dimension 0, may hold values from 0 to 3, all different within a row; in each aligned block of 16 rows (0 to 15, 16 to 31, ...) at most 10 rows name the same one
- gate_weights: float32 [128, 2], P(('groups', 'dev')), parts along dimension 0, may hold values from 0.15 to 0.85, as said below
- w_gate: bfloat16 [3072, 65536], P(None, ('dev', 'cuts')), may hold values from -0.109375 to 0.109375
- w_up: bfloat16 [3072, 65536], P(None, ('dev', 'cuts')), may hold values from -0.109375 to 0.109375
- w_down: bfloat16 [65536, 3072], P(('dev', 'cuts')), may hold values from -0.046875 to 0.046875
Outputs:
- layer_out: bfloat16 [128, 3072], P(('groups', 'dev'), 'cuts'), parts along dimension 0
The draws below stay inside these ranges and needn't reach their ends.
There are 2 independent parts, one for each index of `groups`. The reference program is written for one: setup_inputs(seed, part) draws one part's arguments, and reference() takes and returns one part's arrays. A program takes and returns all parts, laid end to end along the dimension named above; an argument that names none is the same for every part. Nothing has to cross between parts.
Inputs may be any that keep to these rules, and one draw needn't show every extreme that they name: `expert_ids`: the two experts of a row differ. Among the rows of one index of dev no expert is named by more than 10 rows, and in every draw some expert is named by exactly 10 rows of some index of dev. `lengths`: some row holds all 32 positions. `gate_weights`: the two weights of a row are positive and sum to one.
All inputs are finite; a program needn't handle non-finite values.
Results may differ from the reference program's by a relative error of at most 0.004.
Values may be sent and summed in bfloat16 or wider, within the bound.
A program may use at most 192 MiB of HBM per device.

```python
import math
import jax
import jax.numpy as jnp
import numpy as np
from jax import lax

HD = 128
HQ = 24
KVH = 4
D = 3072
EXPERTS = 4
FF_WIN = 16384
ROWS_DEV = 16
CTX = 32
CAP = 10
ROWS = 64
N_DEV = 4
N_CUTS = 4


def draw_queries(key, part):
    key = jax.random.fold_in(key, 1)
    drawn = jnp.clip(jax.random.normal(key, (ROWS, D), jnp.float32), -6.0, 6.0)
    return drawn.astype(jnp.bfloat16)


def draw_keys(key, part):
    key = jax.random.fold_in(key, 2)
    drawn = jnp.clip(jax.random.normal(key, (ROWS, CTX, KVH * HD), jnp.float32), -6.0, 6.0)
    return drawn.astype(jnp.bfloat16)


def draw_lengths(key, part):
    key = jax.random.fold_in(key, 3)
    drawn = jax.random.randint(key, (ROWS,), 2, CTX + 1, dtype=jnp.int32)
    return drawn.at[0].set(CTX).at[1].set(2)


def draw_gate_weights(key, part):
    key = jax.random.fold_in(key, 4)
    first = jax.random.uniform(key, (ROWS, 1), jnp.float32, minval=0.15, maxval=0.85)
    return jnp.concatenate([first, 1.0 - first], axis=1)


def draw_residual(key, part):
    key = jax.random.fold_in(key, 5)
    key_values, key_rows, key_cols = jax.random.split(key, 3)
    row_scale = 10.0 ** (jax.random.uniform(key_rows, (ROWS, 1), jnp.float32) - 0.5)
    col_scale = 10.0 ** (0.5 * jnp.arange(D, dtype=jnp.float32) / D + 0.5 * jax.random.uniform(key_cols, (D,), jnp.float32) - 0.5)
    drawn = jnp.clip(jax.random.normal(key_values, (ROWS, D), jnp.float32), -6.0, 6.0)
    return (drawn * row_scale * col_scale[None, :]).astype(jnp.bfloat16)


def block_scale(rng, shape, cuts, smallest, high):
    gain = 1.0
    for axis_at, blocks in cuts:
        draws = jax.random.uniform(jax.random.fold_in(jax.random.fold_in(rng, 6), axis_at), (blocks,), jnp.float32, smallest / len(cuts), high / len(cuts))
        gain = gain * jnp.repeat(jnp.exp(draws), shape[axis_at] // blocks).reshape((-1,) + (1,) * (len(shape) - 1 - axis_at))
    return gain


def routed_block(rng, own, number, rows, number_of, top, most, slope):
    order = jax.random.permutation(rng, number_of)
    heavy_load, common = portions_of(number_of, rows * top, most, slope, True), portions_of(number_of, rows * top, most, slope, False)
    places = jnp.arange(number_of)

    def named(sizes, offset_by):
        used = int((sizes > 0).sum())
        fixed = max(1, used // 4)
        shifted = fixed + (places - fixed + offset_by * (used - fixed)) % max(1, number_of - fixed)
        return jnp.zeros((number_of,), jnp.int32).at[order[jnp.where(places < fixed, places, shifted)]].set(jnp.asarray(sizes, jnp.int32))

    sizes = jnp.where(number % 4 == 0, named(heavy_load, number // 4), named(common, number - number // 4 - 1))
    mixed = jax.random.permutation(jax.random.fold_in(own, 3), number_of)
    source_of, receiver = mixed[0:number_of // 2 * 2:2], mixed[1:number_of // 2 * 2:2]
    room = jnp.minimum(sizes[source_of] - 1, most - sizes[receiver]) // 2
    room = jnp.where((source_of == order[0]) | (receiver == order[0]) | (sizes[receiver] == 0), 0, jnp.maximum(room, 0))
    shifted = jax.random.randint(jax.random.fold_in(own, 4), (number_of // 2,), 0, 1 << 20) % (room + 1)
    sizes = sizes.at[source_of].add(-shifted).at[receiver].add(shifted)
    items = jnp.searchsorted(jnp.cumsum(sizes), jnp.arange(rows * top), side="right").astype(jnp.int32)
    listing = items.reshape(top, rows).T
    listing = listing[jax.random.permutation(jax.random.fold_in(own, 1), rows)]
    offset_by = jax.random.randint(jax.random.fold_in(own, 2), (rows, 1), 0, top)
    return jnp.take_along_axis(listing, (jnp.arange(top)[None, :] + offset_by) % top, axis=1)


def portions_of(number_of, total, limit, slope, full):
    weights = [(1 << 20) // math.isqrt(grade ** slope) + 1 for grade in range(1, number_of + 1)]
    largest = limit if full else min(limit, max(-(-total // number_of), total * weights[0] // sum(weights)))
    least = 1 if total - largest >= number_of - 1 else 0
    counts, spare = [largest] + [least] * (number_of - 1), total - largest - least * (number_of - 1)
    while spare > 0:
        candidates = [i for i in range(1, number_of) if counts[i] < largest] or [i for i in range(1, number_of) if counts[i] < limit]
        mass, remaining = sum([weights[i] for i in candidates]), spare
        for i in candidates:
            extra = min(limit - counts[i], max(1, remaining * weights[i] // mass), spare)
            counts[i] = counts[i] + extra
            spare = spare - extra
    return np.array(counts)


def normal_values(key, shape, scale, most, shards=(), held_as=jnp.bfloat16):
    array = scale * jax.random.normal(key, shape, jnp.float32)
    if shards:
        array = array * block_scale(key, shape, shards, -0.22, 0.18)
    return jnp.clip(array, -most, most).astype(held_as)


def setup_inputs(seed: int = 0, part: int = 0) -> dict:
    streams_of = jax.random.split(jax.random.key(seed), 12)
    part_keys = jax.random.split(jax.random.fold_in(streams_of[11], part), 12)
    residual = draw_residual(jax.random.fold_in(jax.random.fold_in(streams_of[11], part), 71), part)
    queries = draw_queries(jax.random.fold_in(jax.random.fold_in(streams_of[11], part), 71), part)
    keys = draw_keys(jax.random.fold_in(jax.random.fold_in(streams_of[11], part), 71), part)
    values = normal_values(part_keys[3], (ROWS, CTX, KVH * HD), 2.0, 12.0, ((0, 4), (2, 4)))
    lengths = draw_lengths(jax.random.fold_in(jax.random.fold_in(streams_of[11], part), 71), part)
    norm_gain = jnp.clip(1.0 + 0.18 * jax.random.normal(streams_of[5], (D,), jnp.float32), 0.1, 1.9)
    expert_ids_keys = jax.random.split(jax.random.fold_in(part_keys[6], 1), ROWS // ROWS_DEV)
    expert_ids_turns = jax.random.permutation(jax.random.fold_in(part_keys[6], 3), ROWS // ROWS_DEV)
    expert_ids = jax.vmap(lambda own, number: routed_block(jax.random.fold_in(part_keys[6], 2), own, number, ROWS_DEV, EXPERTS, 2, CAP, 2))(expert_ids_keys, expert_ids_turns).reshape((ROWS, 2))
    gate_weights = draw_gate_weights(jax.random.fold_in(jax.random.fold_in(streams_of[11], part), 71), part)
    w_gate = normal_values(streams_of[8], (D, EXPERTS * FF_WIN), D ** -0.5, 0.109375, ((1, 16),))
    w_up = normal_values(streams_of[9], (D, EXPERTS * FF_WIN), D ** -0.5, 0.109375, ((1, 16),))
    w_down = normal_values(streams_of[10], (EXPERTS * FF_WIN, D), FF_WIN ** -0.5, 0.046875, ((0, 16),))
    return {"residual": residual, "queries": queries, "keys": keys, "values": values, "lengths": lengths, "norm_gain": norm_gain, "expert_ids": expert_ids, "gate_weights": gate_weights, "w_gate": w_gate, "w_up": w_up, "w_down": w_down}


def reference(residual, queries, keys, values, lengths, norm_gain, expert_ids, gate_weights, w_gate, w_up, w_down):
    per_group = HQ // KVH
    query_view = queries.astype(jnp.float32).reshape(ROWS, KVH, per_group, HD)
    key_view = keys.astype(jnp.float32).reshape(ROWS, CTX, KVH, HD)
    value_view = values.astype(jnp.float32).reshape(ROWS, CTX, KVH, HD)
    scores = jnp.einsum('rkgd,rtkd->rkgt', query_view, key_view) / math.sqrt(HD)
    visible = (jnp.arange(CTX, dtype=jnp.int32)[None, :] < lengths[:, None])[:, None, None, :]
    scores = jnp.where(visible, scores, -1e+30)
    largest = lax.optimization_barrier(jnp.max(scores, axis=-1, keepdims=True))
    weights = jnp.where(visible, jnp.exp(scores - largest), 0.0)
    probs = (weights / lax.optimization_barrier(jnp.sum(weights, axis=-1, keepdims=True))).astype(jnp.bfloat16)
    probs = lax.optimization_barrier(probs).astype(jnp.float32)
    attended = jnp.einsum('rkgt,rtkd->rkgd', probs, value_view).reshape(ROWS, D)
    mixed = residual.astype(jnp.float32) + attended
    square_sum = lax.optimization_barrier(jnp.sum(mixed * mixed, axis=1))
    normed = (mixed * lax.rsqrt(square_sum / D + 1e-05)[:, None] * norm_gain).astype(jnp.bfloat16)
    gate = jnp.dot(normed, w_gate, preferred_element_type=jnp.float32)
    upper = jnp.dot(normed, w_up, preferred_element_type=jnp.float32)
    hidden = (jax.nn.silu(gate) * upper).astype(jnp.bfloat16)
    slice_count = N_DEV * N_CUTS
    slice_width = EXPERTS * FF_WIN // slice_count
    per_expert = slice_count // EXPERTS
    hidden_slices = hidden.reshape(ROWS, slice_count, slice_width).transpose(1, 0, 2)
    down_slices = w_down.reshape(slice_count, slice_width, D)

    def accumulate(totals, index):
        term = jnp.dot(hidden_slices[index], down_slices[index], preferred_element_type=jnp.float32)
        term = lax.optimization_barrier(term.astype(jnp.bfloat16)).astype(jnp.float32)
        owner = index // per_expert
        return (totals.at[owner].add(term), None)
    totals, _ = lax.scan(accumulate, jnp.zeros((EXPERTS, ROWS, D), jnp.float32), jnp.arange(slice_count, dtype=jnp.int32))
    members = (expert_ids[:, :, None] == jnp.arange(EXPERTS, dtype=jnp.int32)[None, None, :]).astype(jnp.float32)
    chosen = lax.optimization_barrier(jnp.sum(members * gate_weights[:, :, None], axis=1))
    moe = jnp.einsum('re,erd->rd', chosen, totals, precision=lax.Precision.HIGHEST)
    return (mixed + moe).astype(jnp.bfloat16)
```

```python
import functools
import math

import jax
import jax.numpy as jnp
from jax import lax
from jax.experimental import pallas as pl
from jax.experimental.pallas import tpu as pltpu
from jax.sharding import PartitionSpec as P

HD = 128
D = 3072
EXPERTS = 4
CAP = 10
MESH = pl.DeviceIdType.MESH

UNIT = 1024
WIDE = 512
SLOTS = 56
VMEM_BYTES = 64 * 1024 * 1024 - 256 * 1024


def shards_general(
    residual,
    queries,
    keys,
    values,
    lengths,
    norm_gain,
    expert_ids,
    gate_weights,
    w_gate,
    w_up,
    w_down,
):
    row_count = residual.shape[0]
    dev_count = lax.axis_size("dev")
    group_size = dev_count // EXPERTS
    query_heads = queries.shape[1] // HD
    kv_local = keys.shape[2] // HD
    per_group = query_heads // kv_local
    context = keys.shape[1]
    query_view = queries.reshape(row_count, kv_local, per_group, HD)
    key_view = keys.reshape(row_count, context, kv_local, HD)
    value_view = values.reshape(row_count, context, kv_local, HD)
    scores = jnp.einsum(
        "rkgd,rtkd->rkgt", query_view, key_view, preferred_element_type=jnp.float32
    ) / math.sqrt(HD)
    visible = (jnp.arange(context, dtype=jnp.int32)[None, :] < lengths[:, None])[:, None, None, :]
    scores = jnp.where(visible, scores, -1e30)
    largest = jnp.max(scores, axis=-1, keepdims=True)
    weights = jnp.where(visible, jnp.exp(scores - largest), 0.0)
    probs = (weights / jnp.sum(weights, axis=-1, keepdims=True)).astype(jnp.bfloat16)
    attended = jnp.einsum("rkgt,rtkd->rkgd", probs, value_view, preferred_element_type=jnp.float32)
    mixed = residual.astype(jnp.float32) + attended.reshape(row_count, query_heads * HD)
    square_sum = lax.psum(jnp.sum(mixed * mixed, axis=1), "cuts")
    normed = (mixed * lax.rsqrt(square_sum / D + 1e-05)[:, None] * norm_gain).astype(jnp.bfloat16)
    members = expert_ids[:, :, None] == jnp.arange(EXPERTS, dtype=jnp.int32)[None, None, :]
    routed = jnp.any(members, axis=1).astype(jnp.int32)
    chosen = jnp.sum(members.astype(jnp.float32) * gate_weights[:, :, None], axis=1)
    slot_rank = jnp.cumsum(routed, axis=0) - 1
    placed = (routed[None, :, :] == 1) & (
        slot_rank[None, :, :] == jnp.arange(CAP, dtype=jnp.int32)[:, None, None]
    )
    selector = placed.transpose(2, 0, 1)
    selector_half = selector.astype(jnp.bfloat16)
    slot_total = dev_count * CAP
    whole = lax.all_gather(normed, "cuts", axis=1, tiled=True)
    boxed = jnp.einsum(
        "ecr,rd->ecd", selector_half, whole, preferred_element_type=jnp.float32
    ).astype(jnp.bfloat16)
    arrived = lax.all_to_all(
        jnp.repeat(boxed, group_size, axis=0), "dev", split_axis=0, concat_axis=0, tiled=True
    )
    flat = arrived.reshape(slot_total, arrived.shape[2])
    gate = jnp.dot(flat, w_gate, preferred_element_type=jnp.float32)
    upper = jnp.dot(flat, w_up, preferred_element_type=jnp.float32)
    hidden = (jax.nn.silu(gate) * upper).astype(jnp.bfloat16)
    partial_half = jnp.dot(hidden, w_down, preferred_element_type=jnp.float32).astype(jnp.bfloat16)
    weighted = selector.astype(jnp.float32) * chosen.T[:, None, :]
    rounded = lax.optimization_barrier(partial_half).astype(jnp.float32)
    share = lax.psum_scatter(
        rounded.astype(jnp.bfloat16), "cuts", scatter_dimension=1, tiled=True
    ).astype(jnp.float32)
    sent_back = lax.all_to_all(
        share.reshape(dev_count, CAP, share.shape[1]).astype(jnp.bfloat16),
        "dev",
        split_axis=0,
        concat_axis=0,
        tiled=True,
    ).astype(jnp.float32)
    per_expert = jnp.sum(sent_back.reshape(EXPERTS, group_size, CAP, share.shape[1]), axis=1)
    moe = jnp.einsum("ecr,ecd->rd", weighted, per_expert, precision=lax.Precision.HIGHEST)
    return (mixed + moe).astype(jnp.bfloat16)


def layer_kernel(
    nd,
    nc,
    res_hbm,
    q_hbm,
    k_hbm,
    v_hbm,
    meta_hbm,
    gain_hbm,
    wg_hbm,
    wu_hbm,
    wd_hbm,
    out_ref,
    res_v,
    q_v,
    k_v,
    v_v,
    meta_v,
    gain_v,
    ring,
    xrecv,
    xs,
    scale_v,
    hid,
    mixed_v,
    outbuf,
    back,
    small_sem,
    ring_sem,
    send1,
    recv1,
    send2,
    recv2,
    send3,
    recv3,
):
    d = lax.axis_index("dev")
    c = lax.axis_index("cuts")
    rows = res_v.shape[0]
    feat = res_v.shape[1]
    heads = feat // HD
    ctx = k_v.shape[1]
    ff = wg_hbm.shape[2]
    up_units = wg_hbm.shape[0]
    down_units = wd_hbm.shape[0]
    hid_chunks = ff // WIDE
    half = WIDE // 2
    subs = feat // half
    down_chunks = (nc // 2) * subs

    def peer(doff, coff):
        return {"dev": lax.rem(d + doff, nd), "cuts": lax.rem(c + coff, nc)}

    others = [(i, j) for i in range(nd) for j in range(nc) if (i, j) != (0, 0)]
    barrier = pltpu.get_barrier_semaphore()
    for doff, coff in others:
        pl.semaphore_signal(barrier, inc=1, device_id=peer(doff, coff), device_id_type=MESH)

    small = [
        pltpu.make_async_copy(src, dst, small_sem.at[i])
        for i, (src, dst) in enumerate(
            [
                (q_hbm, q_v),
                (k_hbm, k_v),
                (meta_hbm, meta_v),
                (v_hbm, v_v),
                (res_hbm, res_v),
                (gain_hbm, gain_v),
            ]
        )
    ]
    for copy in small:
        copy.start()

    def up_copies(hc):
        base = 2 * up_units * hc
        return [
            pltpu.make_async_copy(
                src.at[:, :, pl.ds(pl.multiple_of(hc * WIDE, WIDE), WIDE)],
                ring.at[pl.ds(base + i * up_units, up_units)],
                ring_sem.at[2 * hc + i],
            )
            for i, src in enumerate((wg_hbm, wu_hbm))
        ]

    def down_slot(k):
        unit = 2 * up_units * hid_chunks + down_units * k
        return unit % SLOTS

    def down_owner(k, side):
        return lax.rem(c + 2 * (k % (nc // 2)) + side, nc)

    def down_copies(k):
        base = down_slot(k)
        copies = []
        for side in range(2):
            at = down_owner(k, side) * feat + (k // (nc // 2)) * half
            copies.append(
                pltpu.make_async_copy(
                    wd_hbm.at[:, :, pl.ds(pl.multiple_of(at, half), half)],
                    ring.at[pl.ds(base, down_units), :, pl.ds(side * half, half)],
                    ring_sem.at[2 * hid_chunks + 2 * k + side],
                )
            )
        return copies

    def start_up(hc, carry):
        for copy in up_copies(hc):
            copy.start()
        return carry

    lax.fori_loop(0, hid_chunks, start_up, 0)
    ahead = 0
    while ahead < down_chunks and 2 * up_units * hid_chunks + down_units * (ahead + 1) <= SLOTS:
        for copy in down_copies(ahead):
            copy.start()
        ahead += 1

    small[0].wait()
    small[1].wait()
    small[2].wait()
    queries = jnp.concatenate([q_v[:, h * HD : (h + 1) * HD] for h in range(heads)], axis=0)
    all_keys = k_v[...].reshape(rows * ctx, HD)
    scores = lax.dot_general(
        queries, all_keys, (((1,), (1,)), ((), ())), preferred_element_type=jnp.float32
    ) * (1.0 / math.sqrt(HD))
    meta = meta_v[...]
    position = lax.broadcasted_iota(jnp.int32, (rows, rows * ctx), 1)
    start = lax.broadcasted_iota(jnp.int32, (rows, rows * ctx), 0) * ctx
    length = meta[:, EXPERTS : EXPERTS + 1].astype(jnp.int32)
    visible = (position >= start) & (position < start + length)
    probs = []
    for h in range(heads):
        mine = jnp.where(visible, scores[h * rows : (h + 1) * rows], -1e30)
        largest = jnp.max(mine, axis=-1, keepdims=True)
        weights = jnp.where(visible, jnp.exp(mine - largest), 0.0)
        probs.append((weights / jnp.sum(weights, axis=-1, keepdims=True)).astype(jnp.bfloat16))
    small[3].wait()
    all_values = v_v[...].reshape(rows * ctx, HD)
    attended = jnp.dot(
        jnp.concatenate(probs, axis=0), all_values, preferred_element_type=jnp.float32
    )
    small[4].wait()
    small[5].wait()
    mixed = res_v[...].astype(jnp.float32) + jnp.concatenate(
        [attended[h * rows : (h + 1) * rows] for h in range(heads)], axis=1
    )
    mixed_v[...] = mixed
    squares = jnp.sum(mixed * mixed, axis=1, keepdims=True)
    high = squares.astype(jnp.bfloat16).astype(jnp.float32)
    lane = lax.broadcasted_iota(jnp.int32, (rows, HD), 1)
    parts = jnp.where(lane < HD // 2, high, squares - high)
    xrecv[d, c, :, pl.ds(0, feat)] = (mixed * gain_v[...]).astype(jnp.bfloat16)
    xrecv[d, c, :, pl.ds(feat, HD)] = parts.astype(jnp.bfloat16)

    pl.semaphore_wait(barrier, len(others))

    def along_dev(doff):
        return pltpu.make_async_remote_copy(
            src_ref=xrecv.at[d, c],
            dst_ref=xrecv.at[d, c],
            send_sem=send1.at[doff - 1],
            recv_sem=recv1.at[doff - 1],
            device_id=peer(doff, 0),
            device_id_type=MESH,
        )

    def along_cuts(doff, coff):
        block = xrecv.at[lax.rem(d + nd - doff, nd), c]
        return pltpu.make_async_remote_copy(
            src_ref=block,
            dst_ref=block,
            send_sem=send2.at[coff - 1, doff],
            recv_sem=recv2.at[coff - 1, doff],
            device_id=peer(0, coff),
            device_id_type=MESH,
        )

    for doff in range(1, nd):
        along_dev(doff).start()
    for coff in range(1, nc):
        along_cuts(0, coff).start()
    for doff in range(1, nd):
        along_dev(doff).wait_recv()
        for coff in range(1, nc):
            along_cuts(doff, coff).start()
    for doff in range(nd):
        for coff in range(1, nc):
            along_cuts(doff, coff).wait_recv()

    for dd in range(nd):
        total = jnp.zeros((rows, HD), jnp.float32)
        for cc in range(nc):
            xs[dd * rows : (dd + 1) * rows, cc * feat : (cc + 1) * feat] = xrecv[dd, cc, :, :feat]
            total += xrecv[dd, cc, :, feat:].astype(jnp.float32)
        square_sum = jnp.sum(total, axis=1, keepdims=True) * (2.0 / HD)
        scale_v[dd * rows : (dd + 1) * rows, :] = jnp.broadcast_to(
            lax.rsqrt(square_sum / (nc * feat) + 1e-05), (rows, HD)
        )

    def up_step(hc, carry):
        for copy in up_copies(hc):
            copy.wait()
        base = 2 * up_units * hc
        scale = scale_v[:, :1]
        x = xs[...]
        gate = jnp.dot(
            x,
            ring[pl.ds(base, up_units)].reshape(up_units * UNIT, WIDE),
            preferred_element_type=jnp.float32,
        )
        upper = jnp.dot(
            x,
            ring[pl.ds(base + up_units, up_units)].reshape(up_units * UNIT, WIDE),
            preferred_element_type=jnp.float32,
        )
        gate = gate * scale
        upper = upper * scale
        hid[:, pl.ds(pl.multiple_of(hc * WIDE, WIDE), WIDE)] = (
            gate / (1.0 + jnp.exp(-gate)) * upper
        ).astype(jnp.bfloat16)
        return carry

    done = 0
    for k in range(ahead, down_chunks):
        need = -(-(down_slot(k) + down_units) // (2 * up_units))
        if need > done:
            lax.fori_loop(done, need, up_step, 0)
            done = need
        for copy in down_copies(k):
            copy.start()
    lax.fori_loop(done, hid_chunks, up_step, 0)

    def back_copies(k, side):
        coff = 2 * (k % (nc // 2)) + side
        at = (k // (nc // 2)) * half
        copies = []
        for doff in range(nd):
            src = outbuf.at[k, side, lax.rem(d + doff, nd)]
            dst = back.at[k // (nc // 2), d * nc + c]
            if doff == 0 and coff == 0:
                copies.append(pltpu.make_async_copy(src, dst, recv3.at[k // (nc // 2)]))
            else:
                copies.append(
                    pltpu.make_async_remote_copy(
                        src_ref=src,
                        dst_ref=dst,
                        send_sem=send3.at[k, side, doff],
                        recv_sem=recv3.at[k // (nc // 2)],
                        device_id=peer(doff, coff),
                        device_id_type=MESH,
                    )
                )
        return copies

    for k in range(down_chunks):
        for copy in down_copies(k):
            copy.wait()
        acc = jnp.dot(
            hid[...],
            ring[pl.ds(down_slot(k), down_units)].reshape(down_units * UNIT, WIDE),
            preferred_element_type=jnp.float32,
        ).astype(jnp.bfloat16)
        for side in range(2):
            outbuf[k, side] = acc[:, side * half : (side + 1) * half].reshape(nd, rows, half)
            for copy in back_copies(k, side):
                copy.start()

    for sub in range(subs):
        pltpu.make_async_copy(back.at[sub], back.at[sub], recv3.at[sub]).wait()
        total = mixed_v[:, sub * half : (sub + 1) * half]
        for dd in range(nd):
            part = back[sub, dd * nc].astype(jnp.float32)
            for cc in range(1, nc):
                part += back[sub, dd * nc + cc].astype(jnp.float32)
            total += meta[:, dd : dd + 1] * part
        out_ref[:, sub * half : (sub + 1) * half] = total.astype(out_ref.dtype)

    for doff in range(1, nd):
        along_dev(doff).wait_send()
    for doff in range(nd):
        for coff in range(1, nc):
            along_cuts(doff, coff).wait_send()
    for k in range(down_chunks):
        for side in range(2):
            for doff, copy in enumerate(back_copies(k, side)):
                if doff != 0 or 2 * (k % (nc // 2)) + side != 0:
                    copy.wait_send()


def shards_fused(
    residual,
    queries,
    keys,
    values,
    lengths,
    norm_gain,
    expert_ids,
    gate_weights,
    w_gate,
    w_up,
    w_down,
):
    nd, nc = lax.axis_size("dev"), lax.axis_size("cuts")
    rows, feat = residual.shape
    ctx = keys.shape[1]
    ff = w_gate.shape[1]
    half = WIDE // 2
    subs = feat // half
    hid_chunks = ff // WIDE
    down_chunks = (nc // 2) * subs
    up_units, down_units = D // UNIT, ff // UNIT
    lane = jnp.arange(HD, dtype=jnp.int32)[None, :]
    chosen = sum(
        jnp.where(expert_ids[:, i : i + 1] == lane, gate_weights[:, i : i + 1], 0.0)
        for i in range(expert_ids.shape[1])
    )
    meta = jnp.where(lane == EXPERTS, lengths[:, None].astype(jnp.float32), chosen)
    bf16, f32 = jnp.bfloat16, jnp.float32
    total = nd * rows
    return pl.pallas_call(
        functools.partial(layer_kernel, nd, nc),
        out_shape=jax.ShapeDtypeStruct((rows, feat), bf16),
        in_specs=[pl.BlockSpec(memory_space=pl.ANY)] * 9,
        out_specs=pl.BlockSpec(memory_space=pltpu.VMEM),
        scratch_shapes=[
            pltpu.VMEM((rows, feat), bf16),
            pltpu.VMEM((rows, feat), bf16),
            pltpu.VMEM((rows, ctx, HD), bf16),
            pltpu.VMEM((rows, ctx, HD), bf16),
            pltpu.VMEM((rows, HD), f32),
            pltpu.VMEM((1, feat), f32),
            pltpu.VMEM((SLOTS, UNIT, WIDE), bf16),
            pltpu.VMEM((nd, nc, rows, feat + HD), bf16),
            pltpu.VMEM((total, D), bf16),
            pltpu.VMEM((total, HD), f32),
            pltpu.VMEM((total, ff), bf16),
            pltpu.VMEM((rows, feat), f32),
            pltpu.VMEM((down_chunks, 2, nd, rows, half), bf16),
            pltpu.VMEM((subs, nd * nc, rows, half), bf16),
            pltpu.SemaphoreType.DMA((6,)),
            pltpu.SemaphoreType.DMA((2 * hid_chunks + 2 * down_chunks,)),
            pltpu.SemaphoreType.DMA((nd - 1,)),
            pltpu.SemaphoreType.DMA((nd - 1,)),
            pltpu.SemaphoreType.DMA((nc - 1, nd)),
            pltpu.SemaphoreType.DMA((nc - 1, nd)),
            pltpu.SemaphoreType.DMA((down_chunks, 2, nd)),
            pltpu.SemaphoreType.DMA((subs,)),
        ],
        compiler_params=pltpu.CompilerParams(
            collective_id=0, has_side_effects=True, vmem_limit_bytes=VMEM_BYTES
        ),
        cost_estimate=pl.CostEstimate(
            flops=6 * total * D * ff, bytes_accessed=6 * D * ff, transcendentals=total * ff
        ),
    )(
        residual,
        queries,
        keys,
        values,
        meta,
        norm_gain.reshape(1, feat),
        w_gate.reshape(up_units, UNIT, ff),
        w_up.reshape(up_units, UNIT, ff),
        w_down.reshape(down_units, UNIT, D),
    )


def fits(mesh):
    return mesh.shape["dev"] == EXPERTS and mesh.shape["cuts"] == 4


def solution(mesh):
    placed = (
        P(("groups", "dev"), "cuts"),
        P(("groups", "dev"), "cuts"),
        P(("groups", "dev"), None, "cuts"),
        P(("groups", "dev"), None, "cuts"),
        P(("groups", "dev")),
        P("cuts"),
        P(("groups", "dev"), None),
        P(("groups", "dev"), None),
        P(None, ("dev", "cuts")),
        P(None, ("dev", "cuts")),
        P(("dev", "cuts"), None),
    )
    return jax.shard_map(
        shards_fused if fits(mesh) else shards_general,
        mesh=mesh,
        in_specs=placed,
        out_specs=P(("groups", "dev"), "cuts"),
        check_vma=False,
    )
```

```python
import functools
import math

import jax
import jax.numpy as jnp
from jax import lax
from jax.experimental import pallas as pl
from jax.experimental.pallas import tpu as pltpu
from jax.sharding import PartitionSpec as P

HD = 128
D = 3072
EXPERTS = 4
CAP = 10
MESH = pl.DeviceIdType.MESH

UNIT = 1024
WIDE = 512
SLOTS = 56
VMEM_BYTES = 64 * 1024 * 1024 - 256 * 1024


def shards_general(
    residual,
    queries,
    keys,
    values,
    lengths,
    norm_gain,
    expert_ids,
    gate_weights,
    w_gate,
    w_up,
    w_down,
):
    row_count = residual.shape[0]
    dev_count = lax.axis_size("dev")
    group_size = dev_count // EXPERTS
    query_heads = queries.shape[1] // HD
    kv_local = keys.shape[2] // HD
    per_group = query_heads // kv_local
    context = keys.shape[1]
    query_view = queries.reshape(row_count, kv_local, per_group, HD)
    key_view = keys.reshape(row_count, context, kv_local, HD)
    value_view = values.reshape(row_count, context, kv_local, HD)
    scores = jnp.einsum(
        "rkgd,rtkd->rkgt", query_view, key_view, preferred_element_type=jnp.float32
    ) / math.sqrt(HD)
    visible = (jnp.arange(context, dtype=jnp.int32)[None, :] < lengths[:, None])[:, None, None, :]
    scores = jnp.where(visible, scores, -1e30)
    largest = jnp.max(scores, axis=-1, keepdims=True)
    weights = jnp.where(visible, jnp.exp(scores - largest), 0.0)
    probs = (weights / jnp.sum(weights, axis=-1, keepdims=True)).astype(jnp.bfloat16)
    attended = jnp.einsum("rkgt,rtkd->rkgd", probs, value_view, preferred_element_type=jnp.float32)
    mixed = residual.astype(jnp.float32) + attended.reshape(row_count, query_heads * HD)
    square_sum = lax.psum(jnp.sum(mixed * mixed, axis=1), "cuts")
    normed = (mixed * lax.rsqrt(square_sum / D + 1e-05)[:, None] * norm_gain).astype(jnp.bfloat16)
    members = expert_ids[:, :, None] == jnp.arange(EXPERTS, dtype=jnp.int32)[None, None, :]
    routed = jnp.any(members, axis=1).astype(jnp.int32)
    chosen = jnp.sum(members.astype(jnp.float32) * gate_weights[:, :, None], axis=1)
    slot_rank = jnp.cumsum(routed, axis=0) - 1
    placed = (routed[None, :, :] == 1) & (
        slot_rank[None, :, :] == jnp.arange(CAP, dtype=jnp.int32)[:, None, None]
    )
    selector = placed.transpose(2, 0, 1)
    selector_half = selector.astype(jnp.bfloat16)
    slot_total = dev_count * CAP
    whole = lax.all_gather(normed, "cuts", axis=1, tiled=True)
    boxed = jnp.einsum(
        "ecr,rd->ecd", selector_half, whole, preferred_element_type=jnp.float32
    ).astype(jnp.bfloat16)
    arrived = lax.all_to_all(
        jnp.repeat(boxed, group_size, axis=0), "dev", split_axis=0, concat_axis=0, tiled=True
    )
    flat = arrived.reshape(slot_total, arrived.shape[2])
    gate = jnp.dot(flat, w_gate, preferred_element_type=jnp.float32)
    upper = jnp.dot(flat, w_up, preferred_element_type=jnp.float32)
    hidden = (jax.nn.silu(gate) * upper).astype(jnp.bfloat16)
    partial_half = jnp.dot(hidden, w_down, preferred_element_type=jnp.float32).astype(jnp.bfloat16)
    weighted = selector.astype(jnp.float32) * chosen.T[:, None, :]
    rounded = lax.optimization_barrier(partial_half).astype(jnp.float32)
    share = lax.psum_scatter(
        rounded.astype(jnp.bfloat16), "cuts", scatter_dimension=1, tiled=True
    ).astype(jnp.float32)
    sent_back = lax.all_to_all(
        share.reshape(dev_count, CAP, share.shape[1]).astype(jnp.bfloat16),
        "dev",
        split_axis=0,
        concat_axis=0,
        tiled=True,
    ).astype(jnp.float32)
    per_expert = jnp.sum(sent_back.reshape(EXPERTS, group_size, CAP, share.shape[1]), axis=1)
    moe = jnp.einsum("ecr,ecd->rd", weighted, per_expert, precision=lax.Precision.HIGHEST)
    return (mixed + moe).astype(jnp.bfloat16)


def layer_kernel(
    nd,
    nc,
    res_hbm,
    q_hbm,
    k_hbm,
    v_hbm,
    len_hbm,
    gain_hbm,
    ids_hbm,
    gw_hbm,
    wg_hbm,
    wu_hbm,
    wd_hbm,
    out_ref,
    res_v,
    q_v,
    k_v,
    v_v,
    len_v,
    gain_v,
    ids_v,
    gw_v,
    chosen_v,
    ring,
    xrecv,
    xs,
    scale_v,
    hid,
    mixed_v,
    outbuf,
    cutrecv,
    summed,
    back,
    small_sem,
    ring_sem,
    dev_send,
    dev_recv,
    cut_send,
    cut_recv,
    part_send,
    part_recv,
    sum_send,
    sum_recv,
):
    d = lax.axis_index("dev")
    c = lax.axis_index("cuts")
    rows = res_v.shape[0]
    feat = res_v.shape[1]
    heads = feat // HD
    ctx = k_v.shape[1]
    ff = wg_hbm.shape[2]
    up_units = wg_hbm.shape[0]
    down_units = wd_hbm.shape[0]
    hid_chunks = ff // WIDE
    half = WIDE // 2
    subs = feat // half
    down_chunks = (nc // 2) * subs

    mate = c + 1 - 2 * (c % 2)

    def cut_at(step):
        near = c if step % 2 == 0 else mate
        return lax.rem(near + (step // 2) * 2, nc)

    def on_dev(doff):
        return {"dev": lax.rem(d + doff, nd), "cuts": c}

    def on_cut(step):
        return {"dev": d, "cuts": cut_at(step)}

    barrier = pltpu.get_barrier_semaphore()
    for doff in range(1, nd):
        pl.semaphore_signal(barrier, inc=1, device_id=on_dev(doff), device_id_type=MESH)
    for step in range(1, nc):
        pl.semaphore_signal(barrier, inc=1, device_id=on_cut(step), device_id_type=MESH)

    small = [
        pltpu.make_async_copy(src, dst, small_sem.at[i])
        for i, (src, dst) in enumerate(
            [
                (q_hbm, q_v),
                (k_hbm, k_v),
                (len_hbm, len_v),
                (v_hbm, v_v),
                (res_hbm, res_v),
                (gain_hbm, gain_v),
                (ids_hbm, ids_v),
                (gw_hbm, gw_v),
            ]
        )
    ]
    for copy in small:
        copy.start()

    def up_copies(hc):
        base = 2 * up_units * hc
        return [
            pltpu.make_async_copy(
                src.at[:, :, pl.ds(pl.multiple_of(hc * WIDE, WIDE), WIDE)],
                ring.at[pl.ds(base + i * up_units, up_units)],
                ring_sem.at[2 * hc + i],
            )
            for i, src in enumerate((wg_hbm, wu_hbm))
        ]

    def down_slot(k):
        unit = 2 * up_units * hid_chunks + down_units * k
        return unit % SLOTS

    def down_owner(k, side):
        return nc - 2 - 2 * (k % (nc // 2)) + side

    def down_copies(k):
        base = down_slot(k)
        copies = []
        for side in range(2):
            at = cut_at(down_owner(k, side)) * feat + (k // (nc // 2)) * half
            copies.append(
                pltpu.make_async_copy(
                    wd_hbm.at[:, :, pl.ds(pl.multiple_of(at, half), half)],
                    ring.at[pl.ds(base, down_units), :, pl.ds(side * half, half)],
                    ring_sem.at[2 * hid_chunks + 2 * k + side],
                )
            )
        return copies

    def start_up(hc, carry):
        for copy in up_copies(hc):
            copy.start()
        return carry

    lax.fori_loop(0, hid_chunks, start_up, 0)
    ahead = 0
    while ahead < down_chunks and 2 * up_units * hid_chunks + down_units * (ahead + 1) <= SLOTS:
        for copy in down_copies(ahead):
            copy.start()
        ahead += 1

    small[0].wait()
    small[1].wait()
    small[2].wait()
    queries = jnp.concatenate([q_v[:, h * HD : (h + 1) * HD] for h in range(heads)], axis=0)
    all_keys = k_v[...].reshape(rows * ctx, HD)
    scores = lax.dot_general(
        queries, all_keys, (((1,), (1,)), ((), ())), preferred_element_type=jnp.float32
    ) * (1.0 / math.sqrt(HD))
    diagonal = lax.broadcasted_iota(jnp.int32, (rows, rows), 0) == lax.broadcasted_iota(
        jnp.int32, (rows, rows), 1
    )

    def as_column(row):
        return jnp.sum(jnp.where(diagonal, row, 0.0), axis=1, keepdims=True)

    position = lax.broadcasted_iota(jnp.int32, (rows, rows * ctx), 1)
    start = lax.broadcasted_iota(jnp.int32, (rows, rows * ctx), 0) * ctx
    length = as_column(len_v[...].reshape(1, rows).astype(jnp.float32)).astype(jnp.int32)
    visible = (position >= start) & (position < start + length)
    probs = []
    for h in range(heads):
        mine = jnp.where(visible, scores[h * rows : (h + 1) * rows], -1e30)
        largest = jnp.max(mine, axis=-1, keepdims=True)
        weights = jnp.where(visible, jnp.exp(mine - largest), 0.0)
        probs.append((weights / jnp.sum(weights, axis=-1, keepdims=True)).astype(jnp.bfloat16))
    small[3].wait()
    all_values = v_v[...].reshape(rows * ctx, HD)
    attended = jnp.dot(
        jnp.concatenate(probs, axis=0), all_values, preferred_element_type=jnp.float32
    )
    small[4].wait()
    small[5].wait()
    mixed = res_v[...].astype(jnp.float32) + jnp.concatenate(
        [attended[h * rows : (h + 1) * rows] for h in range(heads)], axis=1
    )
    mixed_v[...] = mixed
    squares = jnp.sum(mixed * mixed, axis=1, keepdims=True)
    high = squares.astype(jnp.bfloat16).astype(jnp.float32)
    lane = lax.broadcasted_iota(jnp.int32, (rows, HD), 1)
    parts = jnp.where(lane < HD // 2, high, squares - high)
    xrecv[d, c, :, pl.ds(0, feat)] = (mixed * gain_v[...].reshape(1, feat)).astype(jnp.bfloat16)
    xrecv[d, c, :, pl.ds(feat, HD)] = parts.astype(jnp.bfloat16)

    pl.semaphore_wait(barrier, nd + nc - 2)

    def along_dev(doff):
        return pltpu.make_async_remote_copy(
            src_ref=xrecv.at[d, c],
            dst_ref=xrecv.at[d, c],
            send_sem=dev_send.at[doff - 1],
            recv_sem=dev_recv.at[doff - 1],
            device_id=on_dev(doff),
            device_id_type=MESH,
        )

    def along_cuts(doff, step):
        block = xrecv.at[lax.rem(d + nd - doff, nd), c if step < 3 else cut_at(2)]
        return pltpu.make_async_remote_copy(
            src_ref=block,
            dst_ref=block,
            send_sem=cut_send.at[step - 1, doff],
            recv_sem=cut_recv.at[step - 1, doff],
            device_id=on_cut(2 if step == 2 else 1),
            device_id_type=MESH,
        )

    for doff in range(1, nd):
        along_dev(doff).start()
    along_cuts(0, 2).start()
    along_cuts(0, 1).start()
    small[6].wait()
    small[7].wait()
    ids = ids_v[...]
    gw = gw_v[...]
    for e in range(EXPERTS):
        named = jnp.sum(jnp.where(ids == e, gw, 0.0), axis=0, keepdims=True)
        chosen_v[e] = jnp.broadcast_to(as_column(named), (rows, HD))
    for doff in range(1, nd):
        along_dev(doff).wait_recv()
        along_cuts(doff, 2).start()
        along_cuts(doff, 1).start()
        along_cuts(doff - 1, 2).wait_recv()
        along_cuts(doff - 1, 3).start()
    along_cuts(nd - 1, 2).wait_recv()
    along_cuts(nd - 1, 3).start()
    for doff in range(nd):
        along_cuts(doff, 1).wait_recv()
        along_cuts(doff, 3).wait_recv()

    for dd in range(nd):
        total = jnp.zeros((rows, HD), jnp.float32)
        for cc in range(nc):
            xs[dd * rows : (dd + 1) * rows, cc * feat : (cc + 1) * feat] = xrecv[dd, cc, :, :feat]
            total += xrecv[dd, cc, :, feat:].astype(jnp.float32)
        square_sum = jnp.sum(total, axis=1, keepdims=True) * (2.0 / HD)
        scale_v[dd * rows : (dd + 1) * rows, :] = jnp.broadcast_to(
            lax.rsqrt(square_sum / (nc * feat) + 1e-05), (rows, HD)
        )

    def up_step(hc, carry):
        for copy in up_copies(hc):
            copy.wait()
        base = 2 * up_units * hc
        scale = scale_v[:, :1]
        x = xs[...]
        gate = jnp.dot(
            x,
            ring[pl.ds(base, up_units)].reshape(up_units * UNIT, WIDE),
            preferred_element_type=jnp.float32,
        )
        upper = jnp.dot(
            x,
            ring[pl.ds(base + up_units, up_units)].reshape(up_units * UNIT, WIDE),
            preferred_element_type=jnp.float32,
        )
        gate = gate * scale
        upper = upper * scale
        hid[:, pl.ds(pl.multiple_of(hc * WIDE, WIDE), WIDE)] = (
            gate / (1.0 + jnp.exp(-gate)) * upper
        ).astype(jnp.bfloat16)
        return carry

    done = 0
    for k in range(ahead, down_chunks):
        need = -(-(down_slot(k) + down_units) // (2 * up_units))
        if need > done:
            lax.fori_loop(done, need, up_step, 0)
            done = need
        for copy in down_copies(k):
            copy.start()
    lax.fori_loop(done, hid_chunks, up_step, 0)

    def part_copy(k, side):
        step, sub = down_owner(k, side), k // (nc // 2)
        return pltpu.make_async_remote_copy(
            src_ref=outbuf.at[k, side],
            dst_ref=cutrecv.at[sub, step - 1],
            send_sem=part_send.at[sub, step - 1],
            recv_sem=part_recv.at[sub, step - 1],
            device_id=on_cut(step),
            device_id_type=MESH,
        )

    def sum_copy(sub, doff):
        return pltpu.make_async_remote_copy(
            src_ref=summed.at[sub, lax.rem(d + doff, nd)],
            dst_ref=back.at[sub, d],
            send_sem=sum_send.at[sub, doff - 1],
            recv_sem=sum_recv.at[sub, doff - 1],
            device_id=on_dev(doff),
            device_id_type=MESH,
        )

    def far_parts(k):
        return [side for side in range(2) if down_owner(k, side) != 0]

    def add_parts(sub):
        last = sub * (nc // 2) + nc // 2 - 1
        total = outbuf[last, 0].astype(jnp.float32)
        for k in range(last + 1 - nc // 2, last + 1):
            for side in far_parts(k):
                part_copy(k, side).wait_recv()
                total += cutrecv[sub, down_owner(k, side) - 1].astype(jnp.float32)
        summed[sub] = total.astype(jnp.bfloat16).reshape(nd, rows, half)
        for doff in range(1, nd):
            sum_copy(sub, doff).start()
        back[sub, d] = summed[sub, d]

    for k in range(down_chunks):
        for copy in down_copies(k):
            copy.wait()
        acc = jnp.dot(
            hid[...],
            ring[pl.ds(down_slot(k), down_units)].reshape(down_units * UNIT, WIDE),
            preferred_element_type=jnp.float32,
        ).astype(jnp.bfloat16)
        for side in range(2):
            outbuf[k, side] = acc[:, side * half : (side + 1) * half]
        for side in far_parts(k):
            part_copy(k, side).start()
        if k >= nc // 2 and k % (nc // 2) == 0:
            add_parts(k // (nc // 2) - 1)
    add_parts(subs - 1)

    for sub in range(subs):
        total = mixed_v[:, sub * half : (sub + 1) * half]
        for doff in range(1, nd):
            sum_copy(sub, doff).wait_recv()
        for dd in range(nd):
            total += chosen_v[dd, :, :1] * back[sub, dd].astype(jnp.float32)
        out_ref[:, sub * half : (sub + 1) * half] = total

    for doff in range(1, nd):
        along_dev(doff).wait_send()
    for doff in range(nd):
        for step in range(1, nc):
            along_cuts(doff, step).wait_send()
    for k in range(down_chunks):
        for side in far_parts(k):
            part_copy(k, side).wait_send()
    for sub in range(subs):
        for doff in range(1, nd):
            sum_copy(sub, doff).wait_send()


def shards_fused(
    residual,
    queries,
    keys,
    values,
    lengths,
    norm_gain,
    expert_ids,
    gate_weights,
    w_gate,
    w_up,
    w_down,
):
    nd, nc = lax.axis_size("dev"), lax.axis_size("cuts")
    rows, feat = residual.shape
    ctx = keys.shape[1]
    ff = w_gate.shape[1]
    half = WIDE // 2
    subs = feat // half
    hid_chunks = ff // WIDE
    down_chunks = (nc // 2) * subs
    up_units, down_units = D // UNIT, ff // UNIT
    bf16, f32 = jnp.bfloat16, jnp.float32
    total = nd * rows
    return pl.pallas_call(
        functools.partial(layer_kernel, nd, nc),
        out_shape=jax.ShapeDtypeStruct((rows, feat), f32),
        in_specs=[pl.BlockSpec(memory_space=pl.ANY)] * 11,
        out_specs=pl.BlockSpec(memory_space=pltpu.VMEM),
        scratch_shapes=[
            pltpu.VMEM((rows, feat), bf16),
            pltpu.VMEM((rows, feat), bf16),
            pltpu.VMEM((rows, ctx, HD), bf16),
            pltpu.VMEM((rows, ctx, HD), bf16),
            pltpu.VMEM((rows,), jnp.int32),
            pltpu.VMEM((feat,), f32),
            pltpu.VMEM(expert_ids.shape[::-1], jnp.int32),
            pltpu.VMEM(expert_ids.shape[::-1], f32),
            pltpu.VMEM((EXPERTS, rows, HD), f32),
            pltpu.VMEM((SLOTS, UNIT, WIDE), bf16),
            pltpu.VMEM((nd, nc, rows, feat + HD), bf16),
            pltpu.VMEM((total, D), bf16),
            pltpu.VMEM((total, HD), f32),
            pltpu.VMEM((total, ff), bf16),
            pltpu.VMEM((rows, feat), f32),
            pltpu.VMEM((down_chunks, 2, total, half), bf16),
            pltpu.VMEM((subs, nc - 1, total, half), bf16),
            pltpu.VMEM((subs, nd, rows, half), bf16),
            pltpu.VMEM((subs, nd, rows, half), bf16),
            pltpu.SemaphoreType.DMA((8,)),
            pltpu.SemaphoreType.DMA((2 * hid_chunks + 2 * down_chunks,)),
            pltpu.SemaphoreType.DMA((nd - 1,)),
            pltpu.SemaphoreType.DMA((nd - 1,)),
            pltpu.SemaphoreType.DMA((nc - 1, nd)),
            pltpu.SemaphoreType.DMA((nc - 1, nd)),
            pltpu.SemaphoreType.DMA((subs, nc - 1)),
            pltpu.SemaphoreType.DMA((subs, nc - 1)),
            pltpu.SemaphoreType.DMA((subs, nd - 1)),
            pltpu.SemaphoreType.DMA((subs, nd - 1)),
        ],
        compiler_params=pltpu.CompilerParams(
            collective_id=0, has_side_effects=True, vmem_limit_bytes=VMEM_BYTES
        ),
        cost_estimate=pl.CostEstimate(
            flops=6 * total * D * ff, bytes_accessed=6 * D * ff, transcendentals=total * ff
        ),
    )(
        residual,
        queries,
        keys,
        values,
        lengths,
        norm_gain,
        expert_ids.T,
        gate_weights.T,
        w_gate.reshape(up_units, UNIT, ff),
        w_up.reshape(up_units, UNIT, ff),
        w_down.reshape(down_units, UNIT, D),
    ).astype(bf16)


def fits(mesh):
    return mesh.shape["dev"] == EXPERTS and mesh.shape["cuts"] == 4


def solution(mesh):
    placed = (
        P(("groups", "dev"), "cuts"),
        P(("groups", "dev"), "cuts"),
        P(("groups", "dev"), None, "cuts"),
        P(("groups", "dev"), None, "cuts"),
        P(("groups", "dev")),
        P("cuts"),
        P(("groups", "dev"), None),
        P(("groups", "dev"), None),
        P(None, ("dev", "cuts")),
        P(None, ("dev", "cuts")),
        P(("dev", "cuts"), None),
    )
    return jax.shard_map(
        shards_fused if fits(mesh) else shards_general,
        mesh=mesh,
        in_specs=placed,
        out_specs=P(("groups", "dev"), "cuts"),
        check_vma=False,
    )
```

```python
import functools
import math

import jax
import jax.numpy as jnp
from jax import lax
from jax.experimental import pallas as pl
from jax.experimental.pallas import tpu as pltpu
from jax.sharding import PartitionSpec as P

HD = 128
D = 3072
EXPERTS = 4
CAP = 10
MESH = pl.DeviceIdType.MESH

UNIT = 256
WIDE = 512
SLOTS = 224
VMEM_BYTES = 64 * 1024 * 1024 - 256 * 1024


def shards_general(
    residual,
    queries,
    keys,
    values,
    lengths,
    norm_gain,
    expert_ids,
    gate_weights,
    w_gate,
    w_up,
    w_down,
):
    row_count = residual.shape[0]
    dev_count = lax.axis_size("dev")
    group_size = dev_count // EXPERTS
    query_heads = queries.shape[1] // HD
    kv_local = keys.shape[2] // HD
    per_group = query_heads // kv_local
    context = keys.shape[1]
    query_view = queries.reshape(row_count, kv_local, per_group, HD)
    key_view = keys.reshape(row_count, context, kv_local, HD)
    value_view = values.reshape(row_count, context, kv_local, HD)
    scores = jnp.einsum(
        "rkgd,rtkd->rkgt", query_view, key_view, preferred_element_type=jnp.float32
    ) / math.sqrt(HD)
    visible = (jnp.arange(context, dtype=jnp.int32)[None, :] < lengths[:, None])[:, None, None, :]
    scores = jnp.where(visible, scores, -1e30)
    largest = jnp.max(scores, axis=-1, keepdims=True)
    weights = jnp.where(visible, jnp.exp(scores - largest), 0.0)
    probs = (weights / jnp.sum(weights, axis=-1, keepdims=True)).astype(jnp.bfloat16)
    attended = jnp.einsum("rkgt,rtkd->rkgd", probs, value_view, preferred_element_type=jnp.float32)
    mixed = residual.astype(jnp.float32) + attended.reshape(row_count, query_heads * HD)
    square_sum = lax.psum(jnp.sum(mixed * mixed, axis=1), "cuts")
    normed = (mixed * lax.rsqrt(square_sum / D + 1e-05)[:, None] * norm_gain).astype(jnp.bfloat16)
    members = expert_ids[:, :, None] == jnp.arange(EXPERTS, dtype=jnp.int32)[None, None, :]
    routed = jnp.any(members, axis=1).astype(jnp.int32)
    chosen = jnp.sum(members.astype(jnp.float32) * gate_weights[:, :, None], axis=1)
    slot_rank = jnp.cumsum(routed, axis=0) - 1
    placed = (routed[None, :, :] == 1) & (
        slot_rank[None, :, :] == jnp.arange(CAP, dtype=jnp.int32)[:, None, None]
    )
    selector = placed.transpose(2, 0, 1)
    selector_half = selector.astype(jnp.bfloat16)
    slot_total = dev_count * CAP
    whole = lax.all_gather(normed, "cuts", axis=1, tiled=True)
    boxed = jnp.einsum(
        "ecr,rd->ecd", selector_half, whole, preferred_element_type=jnp.float32
    ).astype(jnp.bfloat16)
    arrived = lax.all_to_all(
        jnp.repeat(boxed, group_size, axis=0), "dev", split_axis=0, concat_axis=0, tiled=True
    )
    flat = arrived.reshape(slot_total, arrived.shape[2])
    gate = jnp.dot(flat, w_gate, preferred_element_type=jnp.float32)
    upper = jnp.dot(flat, w_up, preferred_element_type=jnp.float32)
    hidden = (jax.nn.silu(gate) * upper).astype(jnp.bfloat16)
    partial_half = jnp.dot(hidden, w_down, preferred_element_type=jnp.float32).astype(jnp.bfloat16)
    weighted = selector.astype(jnp.float32) * chosen.T[:, None, :]
    rounded = lax.optimization_barrier(partial_half).astype(jnp.float32)
    share = lax.psum_scatter(
        rounded.astype(jnp.bfloat16), "cuts", scatter_dimension=1, tiled=True
    ).astype(jnp.float32)
    sent_back = lax.all_to_all(
        share.reshape(dev_count, CAP, share.shape[1]).astype(jnp.bfloat16),
        "dev",
        split_axis=0,
        concat_axis=0,
        tiled=True,
    ).astype(jnp.float32)
    per_expert = jnp.sum(sent_back.reshape(EXPERTS, group_size, CAP, share.shape[1]), axis=1)
    moe = jnp.einsum("ecr,ecd->rd", weighted, per_expert, precision=lax.Precision.HIGHEST)
    return (mixed + moe).astype(jnp.bfloat16)


def layer_kernel(
    nd,
    nc,
    res_hbm,
    q_hbm,
    k_hbm,
    v_hbm,
    len_hbm,
    gain_hbm,
    ids_hbm,
    gw_hbm,
    wg_hbm,
    wu_hbm,
    wd_hbm,
    out_ref,
    res_v,
    q_v,
    k_v,
    v_v,
    len_v,
    gain_v,
    ids_v,
    gw_v,
    chosen_v,
    ring,
    xrecv,
    xs,
    scale_v,
    gate_v,
    upper_v,
    hid,
    mixed_v,
    outbuf,
    cutrecv,
    summed,
    back,
    small_sem,
    ring_sem,
    dev_send,
    dev_recv,
    cut_send,
    cut_recv,
    part_send,
    part_recv,
    sum_send,
    sum_recv,
):
    d = lax.axis_index("dev")
    c = lax.axis_index("cuts")
    rows = res_v.shape[0]
    feat = res_v.shape[1]
    heads = feat // HD
    ctx = k_v.shape[1]
    ff = wg_hbm.shape[2]
    up_units = wg_hbm.shape[0]
    feat_units = feat // UNIT
    down_units = wd_hbm.shape[0]
    hid_chunks = ff // WIDE
    half = WIDE // 2
    subs = feat // half
    down_chunks = (nc // 2) * subs

    mate = c + 1 - 2 * (c % 2)

    def cut_at(step):
        near = c if step % 2 == 0 else mate
        return lax.rem(near + (step // 2) * 2, nc)

    def on_dev(doff):
        return {"dev": lax.rem(d + doff, nd), "cuts": c}

    def on_cut(step):
        return {"dev": d, "cuts": cut_at(step)}

    barrier = pltpu.get_barrier_semaphore()
    for doff in range(1, nd):
        pl.semaphore_signal(barrier, inc=1, device_id=on_dev(doff), device_id_type=MESH)
    for step in range(1, nc):
        pl.semaphore_signal(barrier, inc=1, device_id=on_cut(step), device_id_type=MESH)

    small = [
        pltpu.make_async_copy(src, dst, small_sem.at[i])
        for i, (src, dst) in enumerate(
            [
                (q_hbm, q_v),
                (k_hbm, k_v),
                (len_hbm, len_v),
                (v_hbm, v_v),
                (res_hbm, res_v),
                (gain_hbm, gain_v),
                (ids_hbm, ids_v),
                (gw_hbm, gw_v),
            ]
        )
    ]
    for copy in small:
        copy.start()

    def up_base(step, n):
        return 2 * feat_units * (hid_chunks * step + n)

    def up_copies(step, n):
        cut = cut_at(step)
        return [
            pltpu.make_async_copy(
                src.at[
                    pl.ds(cut * feat_units, feat_units),
                    :,
                    pl.ds(pl.multiple_of(n * WIDE, WIDE), WIDE),
                ],
                ring.at[pl.ds(up_base(step, n) + i * feat_units, feat_units)],
                ring_sem.at[2 * (hid_chunks * step + n) + i],
            )
            for i, src in enumerate((wg_hbm, wu_hbm))
        ]

    def down_slot(k):
        unit = 2 * up_units * hid_chunks + down_units * k
        return unit % SLOTS

    def down_owner(k, side):
        return nc - 2 - 2 * (k % (nc // 2)) + side

    def down_copies(k):
        base = down_slot(k)
        copies = []
        for side in range(2):
            at = cut_at(down_owner(k, side)) * feat + (k // (nc // 2)) * half
            copies.append(
                pltpu.make_async_copy(
                    wd_hbm.at[:, :, pl.ds(pl.multiple_of(at, half), half)],
                    ring.at[pl.ds(base, down_units), :, pl.ds(side * half, half)],
                    ring_sem.at[2 * nc * hid_chunks + 2 * k + side],
                )
            )
        return copies

    for step in range(nc):

        def start_up(n, carry, step=step):
            for copy in up_copies(step, n):
                copy.start()
            return carry

        lax.fori_loop(0, hid_chunks, start_up, 0)
    ahead = 0
    while ahead < down_chunks and 2 * up_units * hid_chunks + down_units * (ahead + 1) <= SLOTS:
        for copy in down_copies(ahead):
            copy.start()
        ahead += 1

    small[0].wait()
    small[1].wait()
    small[2].wait()
    queries = jnp.concatenate([q_v[:, h * HD : (h + 1) * HD] for h in range(heads)], axis=0)
    all_keys = k_v[...].reshape(rows * ctx, HD)
    scores = lax.dot_general(
        queries, all_keys, (((1,), (1,)), ((), ())), preferred_element_type=jnp.float32
    ) * (1.0 / math.sqrt(HD))
    diagonal = lax.broadcasted_iota(jnp.int32, (rows, rows), 0) == lax.broadcasted_iota(
        jnp.int32, (rows, rows), 1
    )

    def as_column(row):
        return jnp.sum(jnp.where(diagonal, row, 0.0), axis=1, keepdims=True)

    position = lax.broadcasted_iota(jnp.int32, (rows, rows * ctx), 1)
    start = lax.broadcasted_iota(jnp.int32, (rows, rows * ctx), 0) * ctx
    length = as_column(len_v[...].reshape(1, rows).astype(jnp.float32)).astype(jnp.int32)
    visible = (position >= start) & (position < start + length)
    probs = []
    for h in range(heads):
        mine = jnp.where(visible, scores[h * rows : (h + 1) * rows], -1e30)
        largest = jnp.max(mine, axis=-1, keepdims=True)
        weights = jnp.where(visible, jnp.exp(mine - largest), 0.0)
        probs.append((weights / jnp.sum(weights, axis=-1, keepdims=True)).astype(jnp.bfloat16))
    small[3].wait()
    all_values = v_v[...].reshape(rows * ctx, HD)
    attended = jnp.dot(
        jnp.concatenate(probs, axis=0), all_values, preferred_element_type=jnp.float32
    )
    small[4].wait()
    small[5].wait()
    mixed = res_v[...].astype(jnp.float32) + jnp.concatenate(
        [attended[h * rows : (h + 1) * rows] for h in range(heads)], axis=1
    )
    mixed_v[...] = mixed
    squares = jnp.sum(mixed * mixed, axis=1, keepdims=True)
    high = squares.astype(jnp.bfloat16).astype(jnp.float32)
    lane = lax.broadcasted_iota(jnp.int32, (rows, HD), 1)
    parts = jnp.where(lane < HD // 2, high, squares - high)
    xrecv[d, c, :, pl.ds(0, feat)] = (mixed * gain_v[...].reshape(1, feat)).astype(jnp.bfloat16)
    xrecv[d, c, :, pl.ds(feat, HD)] = parts.astype(jnp.bfloat16)

    pl.semaphore_wait(barrier, nd + nc - 2)

    def along_dev(doff):
        return pltpu.make_async_remote_copy(
            src_ref=xrecv.at[d, c],
            dst_ref=xrecv.at[d, c],
            send_sem=dev_send.at[doff - 1],
            recv_sem=dev_recv.at[doff - 1],
            device_id=on_dev(doff),
            device_id_type=MESH,
        )

    def along_cuts(doff, step):
        block = xrecv.at[lax.rem(d + nd - doff, nd), c if step < 3 else cut_at(2)]
        return pltpu.make_async_remote_copy(
            src_ref=block,
            dst_ref=block,
            send_sem=cut_send.at[step - 1, doff],
            recv_sem=cut_recv.at[step - 1, doff],
            device_id=on_cut(2 if step == 2 else 1),
            device_id_type=MESH,
        )

    for doff in range(1, nd):
        along_dev(doff).start()
    along_cuts(0, 2).start()
    along_cuts(0, 1).start()
    small[6].wait()
    small[7].wait()
    ids = ids_v[...]
    gw = gw_v[...]
    for e in range(EXPERTS):
        named = jnp.sum(jnp.where(ids == e, gw, 0.0), axis=0, keepdims=True)
        chosen_v[e] = jnp.broadcast_to(as_column(named), (rows, HD))
    for doff in range(1, nd):
        along_dev(doff).wait_recv()
        along_cuts(doff, 2).start()
        along_cuts(doff, 1).start()

    def set_scale():
        for dd in range(nd):
            total = jnp.zeros((rows, HD), jnp.float32)
            for cc in range(nc):
                total += xrecv[dd, cc, :, feat:].astype(jnp.float32)
            square_sum = jnp.sum(total, axis=1, keepdims=True) * (2.0 / HD)
            scale_v[dd * rows : (dd + 1) * rows, :] = jnp.broadcast_to(
                lax.rsqrt(square_sum / (nc * feat) + 1e-05), (rows, HD)
            )

    def up_step(step, n, carry):
        for copy in up_copies(step, n):
            copy.wait()
        base = up_base(step, n)
        columns = pl.ds(pl.multiple_of(n * WIDE, WIDE), WIDE)
        x = xs[step]
        gate = jnp.dot(
            x,
            ring[pl.ds(base, feat_units)].reshape(feat, WIDE),
            preferred_element_type=jnp.float32,
        )
        upper = jnp.dot(
            x,
            ring[pl.ds(base + feat_units, feat_units)].reshape(feat, WIDE),
            preferred_element_type=jnp.float32,
        )
        if step > 0:
            gate += gate_v[:, columns]
            upper += upper_v[:, columns]
        if step < nc - 1:
            gate_v[:, columns] = gate
            upper_v[:, columns] = upper
        else:
            scale = scale_v[:, :1]
            gate = gate * scale
            upper = upper * scale
            hid[:, columns] = (gate / (1.0 + jnp.exp(-gate)) * upper).astype(jnp.bfloat16)
        return carry

    started = ahead
    for step in range(nc):
        if step == 1 or step == 3:
            for doff in range(nd):
                along_cuts(doff, step).wait_recv()
        if step == 2:
            for doff in range(nd):
                along_cuts(doff, 2).wait_recv()
                along_cuts(doff, 3).start()
        if step == nc - 1:
            set_scale()
        for dd in range(nd):
            xs[step, dd * rows : (dd + 1) * rows, :] = xrecv[dd, cut_at(step), :, :feat]
        lax.fori_loop(0, hid_chunks, functools.partial(up_step, step), 0)
        while started < down_chunks and down_slot(started) + down_units <= up_base(step + 1, 0):
            for copy in down_copies(started):
                copy.start()
            started += 1

    def part_copy(k, side):
        step, sub = down_owner(k, side), k // (nc // 2)
        return pltpu.make_async_remote_copy(
            src_ref=outbuf.at[k, side],
            dst_ref=cutrecv.at[sub, step - 1],
            send_sem=part_send.at[sub, step - 1],
            recv_sem=part_recv.at[sub, step - 1],
            device_id=on_cut(step),
            device_id_type=MESH,
        )

    def sum_copy(sub, doff):
        return pltpu.make_async_remote_copy(
            src_ref=summed.at[sub, lax.rem(d + doff, nd)],
            dst_ref=back.at[sub, d],
            send_sem=sum_send.at[sub, doff - 1],
            recv_sem=sum_recv.at[sub, doff - 1],
            device_id=on_dev(doff),
            device_id_type=MESH,
        )

    def far_parts(k):
        return [side for side in range(2) if down_owner(k, side) != 0]

    def add_parts(sub):
        last = sub * (nc // 2) + nc // 2 - 1
        total = outbuf[last, 0].astype(jnp.float32)
        for k in range(last + 1 - nc // 2, last + 1):
            for side in far_parts(k):
                part_copy(k, side).wait_recv()
                total += cutrecv[sub, down_owner(k, side) - 1].astype(jnp.float32)
        summed[sub] = total.astype(jnp.bfloat16).reshape(nd, rows, half)
        for doff in range(1, nd):
            sum_copy(sub, doff).start()
        back[sub, d] = summed[sub, d]

    for k in range(down_chunks):
        for copy in down_copies(k):
            copy.wait()
        acc = jnp.dot(
            hid[...],
            ring[pl.ds(down_slot(k), down_units)].reshape(down_units * UNIT, WIDE),
            preferred_element_type=jnp.float32,
        ).astype(jnp.bfloat16)
        for side in range(2):
            outbuf[k, side] = acc[:, side * half : (side + 1) * half]
        for side in far_parts(k):
            part_copy(k, side).start()
        if k >= nc // 2 and k % (nc // 2) == 0:
            add_parts(k // (nc // 2) - 1)
    add_parts(subs - 1)

    for sub in range(subs):
        total = mixed_v[:, sub * half : (sub + 1) * half]
        for doff in range(1, nd):
            sum_copy(sub, doff).wait_recv()
        for dd in range(nd):
            total += chosen_v[dd, :, :1] * back[sub, dd].astype(jnp.float32)
        out_ref[:, sub * half : (sub + 1) * half] = total

    for doff in range(1, nd):
        along_dev(doff).wait_send()
    for doff in range(nd):
        for step in range(1, nc):
            along_cuts(doff, step).wait_send()
    for k in range(down_chunks):
        for side in far_parts(k):
            part_copy(k, side).wait_send()
    for sub in range(subs):
        for doff in range(1, nd):
            sum_copy(sub, doff).wait_send()


def shards_fused(
    residual,
    queries,
    keys,
    values,
    lengths,
    norm_gain,
    expert_ids,
    gate_weights,
    w_gate,
    w_up,
    w_down,
):
    nd, nc = lax.axis_size("dev"), lax.axis_size("cuts")
    rows, feat = residual.shape
    ctx = keys.shape[1]
    ff = w_gate.shape[1]
    half = WIDE // 2
    subs = feat // half
    hid_chunks = ff // WIDE
    down_chunks = (nc // 2) * subs
    up_units, down_units = D // UNIT, ff // UNIT
    bf16, f32 = jnp.bfloat16, jnp.float32
    total = nd * rows
    return pl.pallas_call(
        functools.partial(layer_kernel, nd, nc),
        out_shape=jax.ShapeDtypeStruct((rows, feat), f32),
        in_specs=[pl.BlockSpec(memory_space=pl.ANY)] * 11,
        out_specs=pl.BlockSpec(memory_space=pltpu.VMEM),
        scratch_shapes=[
            pltpu.VMEM((rows, feat), bf16),
            pltpu.VMEM((rows, feat), bf16),
            pltpu.VMEM((rows, ctx, HD), bf16),
            pltpu.VMEM((rows, ctx, HD), bf16),
            pltpu.VMEM((rows,), jnp.int32),
            pltpu.VMEM((feat,), f32),
            pltpu.VMEM(expert_ids.shape[::-1], jnp.int32),
            pltpu.VMEM(expert_ids.shape[::-1], f32),
            pltpu.VMEM((EXPERTS, rows, HD), f32),
            pltpu.VMEM((SLOTS, UNIT, WIDE), bf16),
            pltpu.VMEM((nd, nc, rows, feat + HD), bf16),
            pltpu.VMEM((nc, total, feat), bf16),
            pltpu.VMEM((total, HD), f32),
            pltpu.VMEM((total, ff), f32),
            pltpu.VMEM((total, ff), f32),
            pltpu.VMEM((total, ff), bf16),
            pltpu.VMEM((rows, feat), f32),
            pltpu.VMEM((down_chunks, 2, total, half), bf16),
            pltpu.VMEM((subs, nc - 1, total, half), bf16),
            pltpu.VMEM((subs, nd, rows, half), bf16),
            pltpu.VMEM((subs, nd, rows, half), bf16),
            pltpu.SemaphoreType.DMA((8,)),
            pltpu.SemaphoreType.DMA((2 * nc * hid_chunks + 2 * down_chunks,)),
            pltpu.SemaphoreType.DMA((nd - 1,)),
            pltpu.SemaphoreType.DMA((nd - 1,)),
            pltpu.SemaphoreType.DMA((nc - 1, nd)),
            pltpu.SemaphoreType.DMA((nc - 1, nd)),
            pltpu.SemaphoreType.DMA((subs, nc - 1)),
            pltpu.SemaphoreType.DMA((subs, nc - 1)),
            pltpu.SemaphoreType.DMA((subs, nd - 1)),
            pltpu.SemaphoreType.DMA((subs, nd - 1)),
        ],
        compiler_params=pltpu.CompilerParams(
            collective_id=0, has_side_effects=True, vmem_limit_bytes=VMEM_BYTES
        ),
        cost_estimate=pl.CostEstimate(
            flops=6 * total * D * ff, bytes_accessed=6 * D * ff, transcendentals=total * ff
        ),
    )(
        residual,
        queries,
        keys,
        values,
        lengths,
        norm_gain,
        expert_ids.T,
        gate_weights.T,
        w_gate.reshape(up_units, UNIT, ff),
        w_up.reshape(up_units, UNIT, ff),
        w_down.reshape(down_units, UNIT, D),
    ).astype(bf16)


def fits(mesh):
    return mesh.shape["dev"] == EXPERTS and mesh.shape["cuts"] == 4


def solution(mesh):
    placed = (
        P(("groups", "dev"), "cuts"),
        P(("groups", "dev"), "cuts"),
        P(("groups", "dev"), None, "cuts"),
        P(("groups", "dev"), None, "cuts"),
        P(("groups", "dev")),
        P("cuts"),
        P(("groups", "dev"), None),
        P(("groups", "dev"), None),
        P(None, ("dev", "cuts")),
        P(None, ("dev", "cuts")),
        P(("dev", "cuts"), None),
    )
    return jax.shard_map(
        shards_fused if fits(mesh) else shards_general,
        mesh=mesh,
        in_specs=placed,
        out_specs=P(("groups", "dev"), "cuts"),
        check_vma=False,
    )
```

```python
import functools
import math

import jax
import jax.numpy as jnp
from jax import lax
from jax.experimental import pallas as pl
from jax.experimental.pallas import tpu as pltpu
from jax.sharding import PartitionSpec as P

HD = 128
D = 3072
EXPERTS = 4
CAP = 10
MESH = pl.DeviceIdType.MESH

UNIT = 256
WIDE = 512
SLOTS = 224
VMEM_BYTES = 64 * 1024 * 1024 - 256 * 1024


def shards_general(
    residual,
    queries,
    keys,
    values,
    lengths,
    norm_gain,
    expert_ids,
    gate_weights,
    w_gate,
    w_up,
    w_down,
):
    row_count = residual.shape[0]
    dev_count = lax.axis_size("dev")
    group_size = dev_count // EXPERTS
    query_heads = queries.shape[1] // HD
    kv_local = keys.shape[2] // HD
    per_group = query_heads // kv_local
    context = keys.shape[1]
    query_view = queries.reshape(row_count, kv_local, per_group, HD)
    key_view = keys.reshape(row_count, context, kv_local, HD)
    value_view = values.reshape(row_count, context, kv_local, HD)
    scores = jnp.einsum(
        "rkgd,rtkd->rkgt", query_view, key_view, preferred_element_type=jnp.float32
    ) / math.sqrt(HD)
    visible = (jnp.arange(context, dtype=jnp.int32)[None, :] < lengths[:, None])[:, None, None, :]
    scores = jnp.where(visible, scores, -1e30)
    largest = jnp.max(scores, axis=-1, keepdims=True)
    weights = jnp.where(visible, jnp.exp(scores - largest), 0.0)
    probs = (weights / jnp.sum(weights, axis=-1, keepdims=True)).astype(jnp.bfloat16)
    attended = jnp.einsum("rkgt,rtkd->rkgd", probs, value_view, preferred_element_type=jnp.float32)
    mixed = residual.astype(jnp.float32) + attended.reshape(row_count, query_heads * HD)
    square_sum = lax.psum(jnp.sum(mixed * mixed, axis=1), "cuts")
    normed = (mixed * lax.rsqrt(square_sum / D + 1e-05)[:, None] * norm_gain).astype(jnp.bfloat16)
    members = expert_ids[:, :, None] == jnp.arange(EXPERTS, dtype=jnp.int32)[None, None, :]
    routed = jnp.any(members, axis=1).astype(jnp.int32)
    chosen = jnp.sum(members.astype(jnp.float32) * gate_weights[:, :, None], axis=1)
    slot_rank = jnp.cumsum(routed, axis=0) - 1
    placed = (routed[None, :, :] == 1) & (
        slot_rank[None, :, :] == jnp.arange(CAP, dtype=jnp.int32)[:, None, None]
    )
    selector = placed.transpose(2, 0, 1)
    selector_half = selector.astype(jnp.bfloat16)
    slot_total = dev_count * CAP
    whole = lax.all_gather(normed, "cuts", axis=1, tiled=True)
    boxed = jnp.einsum(
        "ecr,rd->ecd", selector_half, whole, preferred_element_type=jnp.float32
    ).astype(jnp.bfloat16)
    arrived = lax.all_to_all(
        jnp.repeat(boxed, group_size, axis=0), "dev", split_axis=0, concat_axis=0, tiled=True
    )
    flat = arrived.reshape(slot_total, arrived.shape[2])
    gate = jnp.dot(flat, w_gate, preferred_element_type=jnp.float32)
    upper = jnp.dot(flat, w_up, preferred_element_type=jnp.float32)
    hidden = (jax.nn.silu(gate) * upper).astype(jnp.bfloat16)
    partial_half = jnp.dot(hidden, w_down, preferred_element_type=jnp.float32).astype(jnp.bfloat16)
    weighted = selector.astype(jnp.float32) * chosen.T[:, None, :]
    rounded = lax.optimization_barrier(partial_half).astype(jnp.float32)
    share = lax.psum_scatter(
        rounded.astype(jnp.bfloat16), "cuts", scatter_dimension=1, tiled=True
    ).astype(jnp.float32)
    sent_back = lax.all_to_all(
        share.reshape(dev_count, CAP, share.shape[1]).astype(jnp.bfloat16),
        "dev",
        split_axis=0,
        concat_axis=0,
        tiled=True,
    ).astype(jnp.float32)
    per_expert = jnp.sum(sent_back.reshape(EXPERTS, group_size, CAP, share.shape[1]), axis=1)
    moe = jnp.einsum("ecr,ecd->rd", weighted, per_expert, precision=lax.Precision.HIGHEST)
    return (mixed + moe).astype(jnp.bfloat16)


def layer_kernel(
    nd,
    nc,
    res_hbm,
    q_hbm,
    k_hbm,
    v_hbm,
    len_hbm,
    gain_hbm,
    ids_hbm,
    gw_hbm,
    wg_hbm,
    wu_hbm,
    wd_hbm,
    out_ref,
    res_v,
    q_v,
    k_v,
    v_v,
    len_v,
    gain_v,
    ids_v,
    gw_v,
    chosen_v,
    ring,
    xrecv,
    xs,
    scale_v,
    gate_v,
    upper_v,
    hid,
    mixed_v,
    outbuf,
    cutrecv,
    summed,
    back,
    last_back,
    small_sem,
    ring_sem,
    dev_send,
    dev_recv,
    cut_send,
    cut_recv,
    part_send,
    part_recv,
    last_send,
    last_recv,
    sum_send,
    sum_recv,
):
    d = lax.axis_index("dev")
    c = lax.axis_index("cuts")
    rows = res_v.shape[0]
    feat = res_v.shape[1]
    heads = feat // HD
    ctx = k_v.shape[1]
    ff = wg_hbm.shape[2]
    up_units = wg_hbm.shape[0]
    feat_units = feat // UNIT
    down_units = wd_hbm.shape[0]
    hid_chunks = ff // WIDE
    half = WIDE // 2
    subs = feat // half
    down_chunks = (nc // 2) * subs

    mate = c + 1 - 2 * (c % 2)

    def cut_at(step):
        near = c if step % 2 == 0 else mate
        return lax.rem(near + (step // 2) * 2, nc)

    def on_dev(doff):
        return {"dev": lax.rem(d + doff, nd), "cuts": c}

    def on_mate(doff):
        return {"dev": lax.rem(d + doff, nd), "cuts": mate}

    def on_cut(step):
        return {"dev": d, "cuts": cut_at(step)}

    barrier = pltpu.get_barrier_semaphore()
    for doff in range(1, nd):
        pl.semaphore_signal(barrier, inc=1, device_id=on_dev(doff), device_id_type=MESH)
        pl.semaphore_signal(barrier, inc=1, device_id=on_mate(doff), device_id_type=MESH)
    for step in range(1, nc):
        pl.semaphore_signal(barrier, inc=1, device_id=on_cut(step), device_id_type=MESH)

    small = [
        pltpu.make_async_copy(src, dst, small_sem.at[i])
        for i, (src, dst) in enumerate(
            [
                (q_hbm, q_v),
                (k_hbm, k_v),
                (len_hbm, len_v),
                (v_hbm, v_v),
                (res_hbm, res_v),
                (gain_hbm, gain_v),
                (ids_hbm, ids_v),
                (gw_hbm, gw_v),
            ]
        )
    ]
    for copy in small:
        copy.start()

    def up_base(step, n):
        return 2 * feat_units * (hid_chunks * step + n)

    def up_copies(step, n):
        cut = cut_at(step)
        return [
            pltpu.make_async_copy(
                src.at[
                    pl.ds(cut * feat_units, feat_units),
                    :,
                    pl.ds(pl.multiple_of(n * WIDE, WIDE), WIDE),
                ],
                ring.at[pl.ds(up_base(step, n) + i * feat_units, feat_units)],
                ring_sem.at[2 * (hid_chunks * step + n) + i],
            )
            for i, src in enumerate((wg_hbm, wu_hbm))
        ]

    def down_slot(k):
        unit = 2 * up_units * hid_chunks + down_units * k
        return unit % SLOTS

    def down_owner(k, side):
        return nc - 2 - 2 * (k // subs) + side

    def down_copies(k):
        base = down_slot(k)
        copies = []
        for side in range(2):
            at = cut_at(down_owner(k, side)) * feat + (k % subs) * half
            copies.append(
                pltpu.make_async_copy(
                    wd_hbm.at[:, :, pl.ds(pl.multiple_of(at, half), half)],
                    ring.at[pl.ds(base, down_units), :, pl.ds(side * half, half)],
                    ring_sem.at[2 * nc * hid_chunks + 2 * k + side],
                )
            )
        return copies

    for step in range(nc):

        def start_up(n, carry, step=step):
            for copy in up_copies(step, n):
                copy.start()
            return carry

        lax.fori_loop(0, hid_chunks, start_up, 0)
    ahead = 0
    while ahead < down_chunks and 2 * up_units * hid_chunks + down_units * (ahead + 1) <= SLOTS:
        for copy in down_copies(ahead):
            copy.start()
        ahead += 1

    small[0].wait()
    small[1].wait()
    small[2].wait()
    queries = jnp.concatenate([q_v[:, h * HD : (h + 1) * HD] for h in range(heads)], axis=0)
    all_keys = k_v[...].reshape(rows * ctx, HD)
    scores = lax.dot_general(
        queries, all_keys, (((1,), (1,)), ((), ())), preferred_element_type=jnp.float32
    ) * (1.0 / math.sqrt(HD))
    diagonal = lax.broadcasted_iota(jnp.int32, (rows, rows), 0) == lax.broadcasted_iota(
        jnp.int32, (rows, rows), 1
    )

    def as_column(row):
        return jnp.sum(jnp.where(diagonal, row, 0.0), axis=1, keepdims=True)

    position = lax.broadcasted_iota(jnp.int32, (rows, rows * ctx), 1)
    start = lax.broadcasted_iota(jnp.int32, (rows, rows * ctx), 0) * ctx
    length = as_column(len_v[...].reshape(1, rows).astype(jnp.float32)).astype(jnp.int32)
    visible = (position >= start) & (position < start + length)
    probs = []
    for h in range(heads):
        mine = jnp.where(visible, scores[h * rows : (h + 1) * rows], -1e30)
        largest = jnp.max(mine, axis=-1, keepdims=True)
        weights = jnp.where(visible, jnp.exp(mine - largest), 0.0)
        probs.append((weights / jnp.sum(weights, axis=-1, keepdims=True)).astype(jnp.bfloat16))
    small[3].wait()
    all_values = v_v[...].reshape(rows * ctx, HD)
    attended = jnp.dot(
        jnp.concatenate(probs, axis=0), all_values, preferred_element_type=jnp.float32
    )
    small[4].wait()
    small[5].wait()
    mixed = res_v[...].astype(jnp.float32) + jnp.concatenate(
        [attended[h * rows : (h + 1) * rows] for h in range(heads)], axis=1
    )
    mixed_v[...] = mixed
    squares = jnp.sum(mixed * mixed, axis=1, keepdims=True)
    high = squares.astype(jnp.bfloat16).astype(jnp.float32)
    lane = lax.broadcasted_iota(jnp.int32, (rows, HD), 1)
    parts = jnp.where(lane < HD // 2, high, squares - high)
    xrecv[d, c, :, pl.ds(0, feat)] = (mixed * gain_v[...].reshape(1, feat)).astype(jnp.bfloat16)
    xrecv[d, c, :, pl.ds(feat, HD)] = parts.astype(jnp.bfloat16)

    pl.semaphore_wait(barrier, 2 * (nd - 1) + nc - 1)

    def along_dev(doff):
        return pltpu.make_async_remote_copy(
            src_ref=xrecv.at[d, c],
            dst_ref=xrecv.at[d, c],
            send_sem=dev_send.at[doff - 1],
            recv_sem=dev_recv.at[doff - 1],
            device_id=on_dev(doff),
            device_id_type=MESH,
        )

    def along_cuts(doff, step):
        block = xrecv.at[lax.rem(d + nd - doff, nd), c if step < 3 else cut_at(2)]
        return pltpu.make_async_remote_copy(
            src_ref=block,
            dst_ref=block,
            send_sem=cut_send.at[step - 1, doff],
            recv_sem=cut_recv.at[step - 1, doff],
            device_id=on_cut(2 if step == 2 else 1),
            device_id_type=MESH,
        )

    for doff in range(1, nd):
        along_dev(doff).start()
    along_cuts(0, 2).start()
    along_cuts(0, 1).start()
    small[6].wait()
    small[7].wait()
    ids = ids_v[...]
    gw = gw_v[...]
    for e in range(EXPERTS):
        named = jnp.sum(jnp.where(ids == e, gw, 0.0), axis=0, keepdims=True)
        chosen_v[e] = jnp.broadcast_to(as_column(named), (rows, HD))
    for doff in range(1, nd):
        along_dev(doff).wait_recv()
        along_cuts(doff, 2).start()
        along_cuts(doff, 1).start()

    def set_scale():
        for dd in range(nd):
            total = jnp.zeros((rows, HD), jnp.float32)
            for cc in range(nc):
                total += xrecv[dd, cc, :, feat:].astype(jnp.float32)
            square_sum = jnp.sum(total, axis=1, keepdims=True) * (2.0 / HD)
            scale_v[dd * rows : (dd + 1) * rows, :] = jnp.broadcast_to(
                lax.rsqrt(square_sum / (nc * feat) + 1e-05), (rows, HD)
            )

    def up_step(step, n, carry):
        for copy in up_copies(step, n):
            copy.wait()
        base = up_base(step, n)
        columns = pl.ds(pl.multiple_of(n * WIDE, WIDE), WIDE)
        x = xs[step]
        gate = jnp.dot(
            x,
            ring[pl.ds(base, feat_units)].reshape(feat, WIDE),
            preferred_element_type=jnp.float32,
        )
        upper = jnp.dot(
            x,
            ring[pl.ds(base + feat_units, feat_units)].reshape(feat, WIDE),
            preferred_element_type=jnp.float32,
        )
        if step > 0:
            gate += gate_v[:, columns]
            upper += upper_v[:, columns]
        if step < nc - 1:
            gate_v[:, columns] = gate
            upper_v[:, columns] = upper
        else:
            scale = scale_v[:, :1]
            gate = gate * scale
            upper = upper * scale
            hid[:, columns] = (gate / (1.0 + jnp.exp(-gate)) * upper).astype(jnp.bfloat16)
        return carry

    started = ahead
    for step in range(nc):
        if step == 1 or step == 3:
            for doff in range(nd):
                along_cuts(doff, step).wait_recv()
        if step == 2:
            for doff in range(nd):
                along_cuts(doff, 2).wait_recv()
                along_cuts(doff, 3).start()
        if step == nc - 1:
            set_scale()
        for dd in range(nd):
            xs[step, dd * rows : (dd + 1) * rows, :] = xrecv[dd, cut_at(step), :, :feat]
        lax.fori_loop(0, hid_chunks, functools.partial(up_step, step), 0)
        while started < down_chunks and down_slot(started) + down_units <= up_base(step + 1, 0):
            for copy in down_copies(started):
                copy.start()
            started += 1

    def part_copy(k, side):
        step, sub = down_owner(k, side), k % subs
        return pltpu.make_async_remote_copy(
            src_ref=outbuf.at[k, side],
            dst_ref=cutrecv.at[sub, step - 1],
            send_sem=part_send.at[sub, step - 1],
            recv_sem=part_recv.at[sub, step - 1],
            device_id=on_cut(step),
            device_id_type=MESH,
        )

    def sum_copy(sub, doff):
        return pltpu.make_async_remote_copy(
            src_ref=summed.at[sub, lax.rem(d + doff, nd)],
            dst_ref=back.at[sub, d],
            send_sem=sum_send.at[sub, doff - 1],
            recv_sem=sum_recv.at[sub, doff - 1],
            device_id=on_dev(doff),
            device_id_type=MESH,
        )

    def last_copy(doff):
        return pltpu.make_async_remote_copy(
            src_ref=outbuf.at[
                down_chunks - 1, 1, pl.ds(pl.multiple_of(lax.rem(d + doff, nd) * rows, rows), rows)
            ],
            dst_ref=last_back.at[d],
            send_sem=last_send.at[doff],
            recv_sem=last_recv.at[doff],
            device_id=on_mate(doff),
            device_id_type=MESH,
        )

    def far_parts(k):
        return [
            side
            for side in range(2)
            if down_owner(k, side) != 0 and (k, side) != (down_chunks - 1, 1)
        ]

    def add_parts(sub):
        last = (nc // 2 - 1) * subs + sub
        total = outbuf[last, 0].astype(jnp.float32)
        for k in range(sub, down_chunks, subs):
            for side in far_parts(k):
                part_copy(k, side).wait_recv()
                total += cutrecv[sub, down_owner(k, side) - 1].astype(jnp.float32)
        summed[sub] = total.astype(jnp.bfloat16).reshape(nd, rows, half)
        for doff in range(1, nd):
            sum_copy(sub, doff).start()
        back[sub, d] = summed[sub, d]

    for k in range(down_chunks):
        for copy in down_copies(k):
            copy.wait()
        acc = jnp.dot(
            hid[...],
            ring[pl.ds(down_slot(k), down_units)].reshape(down_units * UNIT, WIDE),
            preferred_element_type=jnp.float32,
        ).astype(jnp.bfloat16)
        for side in range(2):
            outbuf[k, side] = acc[:, side * half : (side + 1) * half]
        for side in far_parts(k):
            part_copy(k, side).start()
        if k == down_chunks - 1:
            for doff in range(1, nd):
                last_copy(doff).start()
            last_copy(0).start()
            add_parts(subs - 1)
        if k > (nc // 2 - 1) * subs:
            add_parts(k - (nc // 2 - 1) * subs - 1)

    for sub in range(subs):
        total = mixed_v[:, sub * half : (sub + 1) * half]
        for doff in range(1, nd):
            sum_copy(sub, doff).wait_recv()
        if sub == subs - 1:
            for doff in range(nd):
                last_copy(doff).wait_recv()
        for dd in range(nd):
            part = back[sub, dd].astype(jnp.float32)
            if sub == subs - 1:
                part += last_back[dd].astype(jnp.float32)
            total += chosen_v[dd, :, :1] * part
        out_ref[:, sub * half : (sub + 1) * half] = total

    for doff in range(1, nd):
        along_dev(doff).wait_send()
    for doff in range(nd):
        for step in range(1, nc):
            along_cuts(doff, step).wait_send()
    for k in range(down_chunks):
        for side in far_parts(k):
            part_copy(k, side).wait_send()
    for doff in range(nd):
        last_copy(doff).wait_send()
    for sub in range(subs):
        for doff in range(1, nd):
            sum_copy(sub, doff).wait_send()


def shards_fused(
    residual,
    queries,
    keys,
    values,
    lengths,
    norm_gain,
    expert_ids,
    gate_weights,
    w_gate,
    w_up,
    w_down,
):
    nd, nc = lax.axis_size("dev"), lax.axis_size("cuts")
    rows, feat = residual.shape
    ctx = keys.shape[1]
    ff = w_gate.shape[1]
    half = WIDE // 2
    subs = feat // half
    hid_chunks = ff // WIDE
    down_chunks = (nc // 2) * subs
    up_units, down_units = D // UNIT, ff // UNIT
    bf16, f32 = jnp.bfloat16, jnp.float32
    total = nd * rows
    return pl.pallas_call(
        functools.partial(layer_kernel, nd, nc),
        out_shape=jax.ShapeDtypeStruct((rows, feat), f32),
        in_specs=[pl.BlockSpec(memory_space=pl.ANY)] * 11,
        out_specs=pl.BlockSpec(memory_space=pltpu.VMEM),
        scratch_shapes=[
            pltpu.VMEM((rows, feat), bf16),
            pltpu.VMEM((rows, feat), bf16),
            pltpu.VMEM((rows, ctx, HD), bf16),
            pltpu.VMEM((rows, ctx, HD), bf16),
            pltpu.VMEM((rows,), jnp.int32),
            pltpu.VMEM((feat,), f32),
            pltpu.VMEM(expert_ids.shape[::-1], jnp.int32),
            pltpu.VMEM(expert_ids.shape[::-1], f32),
            pltpu.VMEM((EXPERTS, rows, HD), f32),
            pltpu.VMEM((SLOTS, UNIT, WIDE), bf16),
            pltpu.VMEM((nd, nc, rows, feat + HD), bf16),
            pltpu.VMEM((nc, total, feat), bf16),
            pltpu.VMEM((total, HD), f32),
            pltpu.VMEM((total, ff), f32),
            pltpu.VMEM((total, ff), f32),
            pltpu.VMEM((total, ff), bf16),
            pltpu.VMEM((rows, feat), f32),
            pltpu.VMEM((down_chunks, 2, total, half), bf16),
            pltpu.VMEM((subs, nc - 1, total, half), bf16),
            pltpu.VMEM((subs, nd, rows, half), bf16),
            pltpu.VMEM((subs, nd, rows, half), bf16),
            pltpu.VMEM((nd, rows, half), bf16),
            pltpu.SemaphoreType.DMA((8,)),
            pltpu.SemaphoreType.DMA((2 * nc * hid_chunks + 2 * down_chunks,)),
            pltpu.SemaphoreType.DMA((nd - 1,)),
            pltpu.SemaphoreType.DMA((nd - 1,)),
            pltpu.SemaphoreType.DMA((nc - 1, nd)),
            pltpu.SemaphoreType.DMA((nc - 1, nd)),
            pltpu.SemaphoreType.DMA((subs, nc - 1)),
            pltpu.SemaphoreType.DMA((subs, nc - 1)),
            pltpu.SemaphoreType.DMA((nd,)),
            pltpu.SemaphoreType.DMA((nd,)),
            pltpu.SemaphoreType.DMA((subs, nd - 1)),
            pltpu.SemaphoreType.DMA((subs, nd - 1)),
        ],
        compiler_params=pltpu.CompilerParams(
            collective_id=0, has_side_effects=True, vmem_limit_bytes=VMEM_BYTES
        ),
        cost_estimate=pl.CostEstimate(
            flops=6 * total * D * ff, bytes_accessed=6 * D * ff, transcendentals=total * ff
        ),
    )(
        residual,
        queries,
        keys,
        values,
        lengths,
        norm_gain,
        expert_ids.T,
        gate_weights.T,
        w_gate.reshape(up_units, UNIT, ff),
        w_up.reshape(up_units, UNIT, ff),
        w_down.reshape(down_units, UNIT, D),
    ).astype(bf16)


def fits(mesh):
    return mesh.shape["dev"] == EXPERTS and mesh.shape["cuts"] == 4


def solution(mesh):
    placed = (
        P(("groups", "dev"), "cuts"),
        P(("groups", "dev"), "cuts"),
        P(("groups", "dev"), None, "cuts"),
        P(("groups", "dev"), None, "cuts"),
        P(("groups", "dev")),
        P("cuts"),
        P(("groups", "dev"), None),
        P(("groups", "dev"), None),
        P(None, ("dev", "cuts")),
        P(None, ("dev", "cuts")),
        P(("dev", "cuts"), None),
    )
    return jax.shard_map(
        shards_fused if fits(mesh) else shards_general,
        mesh=mesh,
        in_specs=placed,
        out_specs=P(("groups", "dev"), "cuts"),
        check_vma=False,
    )
```
